32 devices in a mesh: seq: 8 (over z, x), user: 4 (over y, core).
Axes of the slice: x: 2, y: 2, z: 4, core: 2. Of those that a mesh axis runs over, the one named last changes fastest.
Arguments:
- query: bfloat16 [4, 4096, 512], P('user', 'seq'), may hold values from -6 to 6
- key: bfloat16 [4, 4096, 512], P('user', 'seq'), may hold values from -6 to 6
- value: bfloat16 [4, 4096, 512], P('user', 'seq'), may hold values from -6 to 6
- gate: bfloat16 [4, 4096, 512], P('user', 'seq'), may hold values from -6 to 6
- history: bfloat16 [4, 4096, 128], P('user', 'seq'), may hold values from -6 to 6
- w_out: bfloat16 [512, 128], replicated, may hold values from -0.25 to 0.25
- table: bfloat16 [131072, 128], P(('seq', 'user')), may hold values from -0.5 to 0.5
- item_owner: int32 [4, 4096, 5], P('user', 'seq'), may hold values from 0 to 31, all different within a row; in each aligned block of 512 rows (0 to 511, 512 to 1023, ..., all dimensions but the last counted through in order) at most 120 rows name the same one
- item_row: int32 [4, 4096, 5], P('user', 'seq'), may hold values from 0 to 4095
- global_blocks: int32 [4, 2], P('user'), may hold values from 0 to 31, as said below
- lengths: int32 [4], replicated, may hold values from 1024 to 4096, as said below
Outputs:
- d_query: bfloat16 [4, 4096, 512], P('user', 'seq')
- d_key: bfloat16 [4, 4096, 512], P('user', 'seq')
- d_value: bfloat16 [4, 4096, 512], P('user', 'seq')
- d_gate: bfloat16 [4, 4096, 512], P('user', 'seq')
- table_grad: float32 [131072, 128], P(('seq', 'user'))
The draws below stay inside these ranges and needn't reach their ends.
Inputs may be any that keep to these rules, and one draw needn't show every extreme that they name: `item_owner`: in the events of one device (512 aligned events of one user), no owner is named by more than 120 entries, a bound that some block reaches; the 5 owners of one event differ. `global_blocks`: the 2 block numbers of one user differ; the first lies among the blocks of the first 512 events. `lengths`: some user's length is 4096.
All inputs are finite; a program needn't handle non-finite values.
Results may differ from the reference program's by a relative error of at most 0.023.
Values may be sent and summed in bfloat16 or wider, within the bound.
A program may use at most 128 MiB of HBM per device.

```python
import math
import jax
import jax.numpy as jnp
import numpy as np
from jax import lax

HEADS = 8
HEAD_DIM = 64
D = 512
E = 128
BLK = 128
GLOB = 2
NEG = 4
LEN_DEV = 512
ROWS_DEV = 4096
SEQ_LEN = 4096
USERS = 4
NBLOCKS = 32
NITEMS = 131072
CAP = 120
DEVICES = 32


def draw_global_blocks(key, part):
    key = jax.random.fold_in(key, 11)
    first_key, second_key, pick_key = jax.random.split(key, 3)
    first = jax.random.randint(first_key, (USERS,), 0, LEN_DEV // BLK)
    offset = jax.random.randint(second_key, (USERS,), 0, NBLOCKS - 1)
    second = (first + 1 + offset) % NBLOCKS
    chosen = jax.random.randint(pick_key, (), 0, USERS)
    picked = jnp.arange(USERS) == chosen
    first = jnp.where(picked, 0, first)
    second = jnp.where(picked, NBLOCKS - 1, second)
    return jnp.stack([first, second], axis=1).astype(jnp.int32)


def draw_lengths(key, part):
    key = jax.random.fold_in(key, 23)
    first, second = jax.random.split(key)
    drawn = jax.random.randint(first, (USERS,), SEQ_LEN // 4, SEQ_LEN + 1)
    chosen = jax.random.randint(second, (), 0, USERS)
    return jnp.where(jnp.arange(USERS) == chosen, SEQ_LEN, drawn).astype(jnp.int32)


def place_ends(values, own_key, least, high):
    longest = values.shape.index(max(values.shape))
    spots = []
    for shift in (0, 1):
        where = [jax.random.randint(jax.random.fold_in(own_key, axis), (), 0, length) for axis, length in enumerate(values.shape)]
        where[longest] = (where[longest] + shift) % values.shape[longest]
        spots.append(tuple(where))
    return values.at[spots[0]].set(least).at[spots[1]].set(high)


def steps_of(key, extent, cuts, least, largest):
    loudness, own = 1.0, jax.random.fold_in(key, 6)
    for axis_at, blocks in cuts:
        steps = jnp.exp(jax.random.uniform(jax.random.fold_in(own, axis_at), (blocks,), jnp.float32, least / len(cuts), largest / len(cuts)))
        loudness = loudness * jnp.repeat(steps, extent[axis_at] // blocks).reshape([-1 if axis == axis_at else 1 for axis in range(len(extent))])
    return loudness


def assign_block(stream_key, own, number, rows, count, top, reach, skew):
    order = jax.random.permutation(stream_key, count)
    heavy_load, ordinary = portions_of(count, rows * top, reach, skew, True), portions_of(count, rows * top, reach, skew, False)
    places = jnp.arange(count)

    def named(tallies, turn):
        used = int((tallies > 0).sum())
        fixed = max(1, used // 4)
        shifted = fixed + (places - fixed + turn * (used - fixed)) % max(1, count - fixed)
        return jnp.zeros((count,), jnp.int32).at[order[jnp.where(places < fixed, places, shifted)]].set(jnp.asarray(tallies, jnp.int32))

    tallies = jnp.where(number % 4 == 0, named(heavy_load, number // 4), named(ordinary, number - number // 4 - 1))
    mixed = jax.random.permutation(jax.random.fold_in(own, 3), count)
    giver, receiver = mixed[0:count // 2 * 2:2], mixed[1:count // 2 * 2:2]
    margin = jnp.minimum(tallies[giver] - 1, reach - tallies[receiver]) // 2
    margin = jnp.where((giver == order[0]) | (receiver == order[0]) | (tallies[receiver] == 0), 0, jnp.maximum(margin, 0))
    shifted = jax.random.randint(jax.random.fold_in(own, 4), (count // 2,), 0, 1 << 20) % (margin + 1)
    tallies = tallies.at[giver].add(-shifted).at[receiver].add(shifted)
    members = jnp.searchsorted(jnp.cumsum(tallies), jnp.arange(rows * top), side="right").astype(jnp.int32)
    table = members.reshape(top, rows).T
    table = table[jax.random.permutation(jax.random.fold_in(own, 1), rows)]
    turn = jax.random.randint(jax.random.fold_in(own, 2), (rows, 1), 0, top)
    return jnp.take_along_axis(table, (jnp.arange(top)[None, :] + turn) % top, axis=1)


def portions_of(amount, total, limit, lean, full):
    portions = [(1 << 20) // math.isqrt(grade ** lean) + 1 for grade in range(1, amount + 1)]
    largest = limit if full else min(limit, max(-(-total // amount), total * portions[0] // sum(portions)))
    least = 1 if total - largest >= amount - 1 else 0
    counts, surplus = [largest] + [least] * (amount - 1), total - largest - least * (amount - 1)
    while surplus > 0:
        movable = [i for i in range(1, amount) if counts[i] < largest] or [i for i in range(1, amount) if counts[i] < limit]
        mass, remaining = sum([portions[i] for i in movable]), surplus
        for i in movable:
            more = min(limit - counts[i], max(1, remaining * portions[i] // mass), surplus)
            counts[i] = counts[i] + more
            surplus = surplus - more
    return np.array(counts)


def gaussian(stream_key, dims, scale, most, cuts=(), kind=jnp.bfloat16):
    loudness = steps_of(stream_key, dims, cuts, -0.22, 0.18) if cuts else 1.0
    values = jax.random.normal(stream_key, dims, jnp.float32) * scale * loudness
    return jnp.minimum(jnp.maximum(values, -most), most).astype(kind)


def setup_inputs(seed: int = 0) -> dict:
    streams_of = jax.random.split(jax.random.key(seed), 12)
    query = gaussian(streams_of[0], (USERS, SEQ_LEN, D), 1.0, 6.0, ((0, 4), (1, 8)))
    key = gaussian(streams_of[1], (USERS, SEQ_LEN, D), 1.0, 6.0, ((0, 4), (1, 8)))
    value = gaussian(streams_of[2], (USERS, SEQ_LEN, D), 1.0, 6.0, ((0, 4), (1, 8)))
    gate = gaussian(streams_of[3], (USERS, SEQ_LEN, D), 1.0, 6.0, ((0, 4), (1, 8)))
    history = gaussian(streams_of[4], (USERS, SEQ_LEN, E), 1.0, 6.0, ((0, 4), (1, 8)))
    w_out = gaussian(streams_of[5], (D, E), D ** -0.5, 0.25)
    table = gaussian(streams_of[6], (NITEMS, E), E ** -0.5, 0.5, ((0, 32),))
    item_owner_keys = jax.random.split(jax.random.fold_in(streams_of[7], 1), USERS * SEQ_LEN // LEN_DEV)
    item_owner_turns = jax.random.permutation(jax.random.fold_in(streams_of[7], 3), USERS * SEQ_LEN // LEN_DEV)
    item_owner = jax.vmap(lambda own, number: assign_block(jax.random.fold_in(streams_of[7], 2), own, number, LEN_DEV, DEVICES, NEG + 1, CAP, 2))(item_owner_keys, item_owner_turns).reshape((USERS, SEQ_LEN, NEG + 1))
    item_row = place_ends(jax.random.randint(streams_of[8], (USERS, SEQ_LEN, NEG + 1), 0, ROWS_DEV), jax.random.fold_in(streams_of[8], 1), 0, ROWS_DEV - 1).astype(jnp.int32)
    global_blocks = draw_global_blocks(jax.random.fold_in(streams_of[11], 71), 0)
    lengths = draw_lengths(jax.random.fold_in(streams_of[11], 71), 0)
    return dict(query=query, key=key, value=value, gate=gate, history=history, w_out=w_out, table=table, item_owner=item_owner, item_row=item_row, global_blocks=global_blocks, lengths=lengths)


def product(form, left, right):
    return jnp.einsum(form, left.astype(jnp.float32), right.astype(jnp.float32), precision=lax.Precision.HIGHEST)

def key_mask(block, gids, length):
    offs = jnp.arange(BLK, dtype=jnp.int32)
    q_pos = block * BLK + offs
    prev_pos = (block - 1) * BLK + offs
    own_pos = block * BLK + offs
    glob_pos = gids[:, None] * BLK + offs[None, :]
    prev_ok = (prev_pos >= 0) & (prev_pos < length)
    own_ok = (own_pos[None, :] <= q_pos[:, None]) & (own_pos[None, :] < length)
    glob_ok = ((gids[:, None] < block - 1) & (glob_pos < length)).reshape(-1)
    mask = jnp.concatenate([jnp.broadcast_to(prev_ok[None, :], (BLK, BLK)), own_ok, jnp.broadcast_to(glob_ok[None, :], (BLK, GLOB * BLK))], axis=1)
    return mask.astype(jnp.float32)

def split_heads(rows):
    return rows.reshape(rows.shape[0], HEADS, HEAD_DIM)

def attend_forward(q_blk, keys, mask):
    width = q_blk.shape[1]
    heads = split_heads(q_blk)
    kk = split_heads(keys[:, :width])
    vv = split_heads(keys[:, width:])
    scores = product('qhd,khd->hqk', heads, kk) * HEAD_DIM ** (-0.5)
    probs = (jax.nn.silu(scores) * mask[None]).astype(jnp.bfloat16)
    return product('hqk,khd->qhd', probs, vv).reshape(q_blk.shape[0], width)

def attend_backward(q_blk, keys, mask, grad_out):
    width = q_blk.shape[1]
    scale = HEAD_DIM ** (-0.5)
    heads = split_heads(q_blk)
    kk = split_heads(keys[:, :width])
    vv = split_heads(keys[:, width:])
    grads = split_heads(grad_out)
    scores = product('qhd,khd->hqk', heads, kk) * scale
    probs = (jax.nn.silu(scores) * mask[None]).astype(jnp.bfloat16)
    d_probs = product('qhd,khd->hqk', grads, vv)
    d_val = product('hqk,qhd->khd', probs, grads)
    sig = jax.nn.sigmoid(scores)
    d_scores = (d_probs * sig * (1.0 + scores * (1.0 - sig)) * mask[None] * scale).astype(jnp.bfloat16)
    d_q = product('hqk,khd->qhd', d_scores, kk)
    d_k = product('hqk,qhd->khd', d_scores, heads)
    count = keys.shape[0]
    return (d_q.reshape(q_blk.shape[0], width), jnp.concatenate([d_k.reshape(count, width), d_val.reshape(count, width)], axis=1))

def middle(attn, gate, history, w_out, emb, valid):
    mean = lax.optimization_barrier(jnp.mean(attn, axis=1, keepdims=True))
    centered = attn - mean
    var = lax.optimization_barrier(jnp.mean(centered * centered, axis=1, keepdims=True))
    inv = lax.rsqrt(var + 1e-05)
    normed = centered * inv
    gate_f = gate.astype(jnp.float32)
    gated = (normed * gate_f).astype(jnp.bfloat16)
    user_vec = product('rd,de->re', gated, w_out) + history.astype(jnp.float32)
    score = product('re,rje->rj', user_vec, emb)
    side = jax.nn.sigmoid(score[:, 1:] - score[:, :1]) * valid[:, None]
    coef = jnp.concatenate([-lax.optimization_barrier(jnp.sum(side, axis=1, keepdims=True)), side], axis=1)
    d_user = product('rj,rje->re', coef, emb).astype(jnp.bfloat16)
    d_emb = coef[:, :, None] * user_vec[:, None, :]
    d_gated = product('re,de->rd', d_user, w_out)
    d_gate = (d_gated * normed).astype(jnp.bfloat16)
    dn = d_gated * gate_f
    d_attn = (dn - lax.optimization_barrier(jnp.mean(dn, axis=1, keepdims=True)) - normed * lax.optimization_barrier(jnp.mean(dn * normed, axis=1, keepdims=True))) * inv
    return (d_attn.astype(jnp.bfloat16), d_gate, d_emb)

def reference(query, key, value, gate, history, w_out, table, item_owner, item_row, global_blocks, lengths):
    nblocks = SEQ_LEN // BLK
    blocks = jnp.arange(nblocks, dtype=jnp.int32)

    def per_user(table_grad, inputs):
        q_all, k_all, v_all, gate_all, hist, owner, row, gids, length = inputs
        width = q_all.shape[1]
        kv = jnp.concatenate([k_all, v_all], axis=1)

        def starts_of(b):
            starts = [jnp.maximum(b - 1, 0) * BLK, b * BLK]
            for index in range(GLOB):
                starts.append(gids[index] * BLK)
            return [s.astype(jnp.int32) for s in starts]

        def keys_of(b):
            return jnp.concatenate([lax.dynamic_slice_in_dim(kv, s, BLK, 0) for s in starts_of(b)], axis=0)

        def forward(b):
            q_blk = lax.dynamic_slice_in_dim(q_all, (b * BLK).astype(jnp.int32), BLK, 0)
            return attend_forward(q_blk, keys_of(b), key_mask(b, gids, length))
        attn = lax.map(forward, blocks).reshape(SEQ_LEN, width)
        ids = (owner * ROWS_DEV + row).astype(jnp.int32)
        emb = table[ids]
        valid = (jnp.arange(SEQ_LEN, dtype=jnp.int32) < length).astype(jnp.float32)
        d_attn, d_gate, d_emb = middle(attn, gate_all, hist, w_out, emb, valid)

        def backward(dkv, b):
            start = (b * BLK).astype(jnp.int32)
            q_blk = lax.dynamic_slice_in_dim(q_all, start, BLK, 0)
            grad_blk = lax.dynamic_slice_in_dim(d_attn, start, BLK, 0)
            d_q, d_keys = attend_backward(q_blk, keys_of(b), key_mask(b, gids, length), grad_blk)
            for index, place in enumerate(starts_of(b)):
                current = lax.dynamic_slice_in_dim(dkv, place, BLK, 0)
                dkv = lax.dynamic_update_slice_in_dim(dkv, current + d_keys[index * BLK:(index + 1) * BLK], place, 0)
            return (dkv, d_q.astype(jnp.bfloat16))
        dkv, d_q = lax.scan(backward, jnp.zeros((SEQ_LEN, 2 * width), jnp.float32), blocks)
        table_grad = table_grad.at[ids.reshape(-1)].add(d_emb.reshape(-1, E))
        outputs = (d_q.reshape(SEQ_LEN, width), dkv[:, :width].astype(jnp.bfloat16), dkv[:, width:].astype(jnp.bfloat16), d_gate)
        return (table_grad, outputs)
    start_grad = jnp.zeros((NITEMS, E), jnp.float32)
    table_grad, (d_query, d_key, d_value, d_gate) = lax.scan(per_user, start_grad, (query, key, value, gate, history, item_owner, item_row, global_blocks, lengths))
    return (d_query, d_key, d_value, d_gate, table_grad)
```

```python
import functools

import jax
import jax.numpy as jnp
from jax import lax
from jax.experimental import pallas as pl
from jax.experimental.pallas import tpu as pltpu
from jax.sharding import PartitionSpec as P

HEADS = 8
HEAD_DIM = 64
BLK = 128
GLOB = 2
PAIR = 2 * HEAD_DIM
HI = 512
F32 = jnp.float32
BF16 = jnp.bfloat16
VMEM = pl.BlockSpec(memory_space=pltpu.VMEM)
SMEM = pl.BlockSpec(memory_space=pltpu.SMEM)
NT = (((1,), (1,)), ((), ()))
TN = (((0,), (0,)), ((), ()))
LIMIT = 50 * 1024 * 1024


def iota(shape, axis):
    return lax.broadcasted_iota(jnp.int32, shape, axis)


def mm(left, right):
    return jnp.dot(left, right, preferred_element_type=F32)


def dg(left, right, dims):
    return lax.dot_general(left, right, dims, preferred_element_type=F32)


def request_kernel(owner_ref, row_ref, slots_ref, req_ref):
    ndev, events = slots_ref.shape
    cap = req_ref.shape[1]
    dev = iota((ndev, events), 0)
    hits = [owner_ref[j : j + 1, :] == dev for j in range(owner_ref.shape[0])]
    named = functools.reduce(jnp.logical_or, hits)
    upper = (iota((events, events), 0) < iota((events, events), 1)).astype(BF16)
    rank = mm(named.astype(BF16), upper)
    slots_ref[...] = jnp.where(named, rank, -1.0)
    high = jnp.zeros((ndev, cap), F32)
    low = jnp.zeros((ndev, cap), F32)
    place = iota((cap, events), 0)
    for j, hit in enumerate(hits):
        slot = jnp.sum(jnp.where(hit, rank, 0.0), axis=0, keepdims=True).astype(jnp.int32)
        chosen = (place == slot).astype(BF16)
        code = row_ref[j : j + 1, :] + 1
        high += dg(jnp.where(hit, (code // 64).astype(F32), 0.0).astype(BF16), chosen, NT)
        low += dg(jnp.where(hit, (code % 64).astype(F32), 0.0).astype(BF16), chosen, NT)
    req_ref[...] = (high * 64.0 + low).astype(jnp.int32) - 1


def gather_kernel(asked_ref, table_ref, out_ref):
    cap, ndev = asked_ref.shape
    width = table_ref.shape[1]
    parts = table_ref.shape[0] // HI
    for d in range(ndev):
        ask = asked_ref[:, d : d + 1]
        part = ask // HI
        chosen = (jnp.broadcast_to(ask - part * HI, (cap, HI)) == iota((cap, HI), 1)).astype(BF16)
        part_b = jnp.broadcast_to(part, (cap, width))
        empty = jnp.broadcast_to(ask, (cap, width)) < 0
        rows = jnp.zeros((cap, width), F32)
        for k in range(parts):
            rows = jnp.where(part_b == k, mm(chosen, table_ref[k * HI : (k + 1) * HI, :]), rows)
        out_ref[d] = jnp.where(empty, 0.0, rows).astype(BF16)


def scatter_kernel(asked_ref, asked_row_ref, inc_ref, out_ref):
    ndev, cap, width = inc_ref.shape
    parts = out_ref.shape[0] // HI
    group = max(1, 512 // cap)
    for first in range(0, ndev, group):
        row = asked_row_ref[:, first * cap : (first + group) * cap]
        chosen = (row % HI == iota((HI, group * cap), 0)).astype(BF16)
        pieces = []
        for d in range(first, first + group):
            part_b = jnp.broadcast_to(asked_ref[:, d : d + 1], (cap, width)) // HI
            inc = inc_ref[d].astype(F32)
            wide = [jnp.where(part_b == k, inc, 0.0).astype(BF16) for k in range(parts)]
            pieces.append(jnp.concatenate(wide, axis=1))
        total = mm(chosen, jnp.concatenate(pieces, axis=0))
        for k in range(parts):
            rows = slice(k * HI, (k + 1) * HI)
            piece = total[:, k * width : (k + 1) * width]
            if first == 0:
                out_ref[rows, :] = piece
            else:
                out_ref[rows, :] += piece


def stack_pair(rows):
    lane = iota(rows.shape, 1)
    zero = jnp.zeros_like(rows)
    return jnp.concatenate(
        [jnp.where(lane < HEAD_DIM, rows, zero), jnp.where(lane < HEAD_DIM, zero, rows)], axis=0
    )


def merge_pair(stacked):
    half = stacked.shape[0] // 2
    lane = iota((half, stacked.shape[1]), 1)
    return jnp.where(lane < HEAD_DIM, stacked[:half], stacked[half:])


def visible(info_ref, b):
    block, length = info_ref[0] + b, info_ref[1]
    query = iota((2 * BLK, BLK), 0) % BLK
    key = iota((2 * BLK, BLK), 1)
    prev = (key + (block - 1) * BLK < length) & (block > 0)
    own = (key <= query) & (key + block * BLK < length)
    globs = [
        (key + info_ref[2 + g] * BLK < length) & (info_ref[2 + g] < block - 1) for g in range(GLOB)
    ]
    return jnp.concatenate([m.astype(F32) for m in [prev, own] + globs], axis=1)


def forward_kernel(info_ref, q_ref, k_ref, v_ref, prev_ref, glob_ref, attn_ref):
    events, width = q_ref.shape
    for b in range(events // BLK):
        rows = slice(b * BLK, (b + 1) * BLK)
        mask = visible(info_ref, b)
        for p in range(width // PAIR):
            cols = slice(p * PAIR, (p + 1) * PAIR)
            vcols = slice(width + p * PAIR, width + (p + 1) * PAIR)
            kk = jnp.concatenate(
                [
                    prev_ref[:, cols] if b == 0 else k_ref[(b - 1) * BLK : b * BLK, cols],
                    k_ref[rows, cols],
                ]
                + [glob_ref[g, :, cols] for g in range(GLOB)],
                axis=0,
            )
            vv = jnp.concatenate(
                [
                    prev_ref[:, vcols] if b == 0 else v_ref[(b - 1) * BLK : b * BLK, cols],
                    v_ref[rows, cols],
                ]
                + [glob_ref[g, :, vcols] for g in range(GLOB)],
                axis=0,
            )
            qs = stack_pair(q_ref[rows, cols]) * HEAD_DIM**-0.5
            scores = dg(qs, kk, NT)
            sig = 0.5 * jnp.tanh(0.5 * scores) + 0.5
            probs = (scores * sig * mask).astype(BF16)
            attn_ref[rows, cols] = merge_pair(mm(probs, vv))


def middle_kernel(
    info_ref, attn_ref, gate_ref, hist_ref, w_ref, ret_ref, slots_ref, owner_ref,
    d_attn_ref, d_gate_ref, out_ref,
):
    ndev, cap, emb = ret_ref.shape
    events = attn_ref.shape[0]
    attn = attn_ref[...]
    centered = attn - jnp.mean(attn, axis=1, keepdims=True)
    inv = lax.rsqrt(jnp.mean(centered * centered, axis=1, keepdims=True) + 1e-05)
    normed = centered * inv
    gate = gate_ref[...].astype(F32)
    user = mm((normed * gate).astype(BF16), w_ref[...]) + hist_ref[...].astype(F32)
    user_hi = user.astype(BF16)
    user_lo = (user - user_hi.astype(F32)).astype(BF16)
    slots = slots_ref[...].astype(jnp.int32)
    place = iota((cap, events), 0)
    score = []
    for d in range(ndev):
        rows = ret_ref[d]
        full = dg(rows, user_hi, NT) + dg(rows, user_lo, NT)
        score.append(
            jnp.sum(jnp.where(place == slots[d : d + 1], full, 0.0), axis=0, keepdims=True)
        )
    score = jnp.concatenate(score, axis=0)
    positive = owner_ref[0:1, :] == iota((ndev, events), 0)
    first = jnp.sum(jnp.where(positive, score, 0.0), axis=0, keepdims=True)
    valid = info_ref[0] * BLK + iota((ndev, events), 1) < info_ref[1]
    side = jnp.where((slots >= 0) & valid & ~positive, jax.nn.sigmoid(score - first), 0.0)
    coef = jnp.where(positive, -jnp.sum(side, axis=0, keepdims=True), side)
    d_user = jnp.zeros((emb, events), F32)
    for d in range(ndev):
        weights = jnp.where(place == slots[d : d + 1], coef[d : d + 1], 0.0).astype(BF16)
        out_ref[d] = mm(weights, user_hi).astype(BF16)
        d_user += dg(ret_ref[d], weights, TN)
    d_gated = dg(d_user.T.astype(BF16), w_ref[...], NT)
    d_gate_ref[...] = (d_gated * normed).astype(BF16)
    dn = d_gated * gate
    d_attn_ref[...] = (
        (
            dn
            - jnp.mean(dn, axis=1, keepdims=True)
            - normed * jnp.mean(dn * normed, axis=1, keepdims=True)
        )
        * inv
    ).astype(BF16)


def backward_kernel(
    info_ref, q_ref, k_ref, v_ref, prev_ref, glob_ref, g_ref,
    dq_ref, dkv_ref, d_prev_ref, d_glob_ref, acc_ref,
):
    events, width = q_ref.shape
    nbd = events // BLK
    for b in range(nbd):
        rows = slice(b * BLK, (b + 1) * BLK)
        before = slice((b - 1) * BLK, b * BLK)
        mask = visible(info_ref, b)
        for p in range(width // PAIR):
            cols = slice(p * PAIR, (p + 1) * PAIR)
            vcols = slice(width + p * PAIR, width + (p + 1) * PAIR)
            kk = jnp.concatenate(
                [prev_ref[:, cols] if b == 0 else k_ref[before, cols], k_ref[rows, cols]]
                + [glob_ref[g, :, cols] for g in range(GLOB)],
                axis=0,
            )
            vv = jnp.concatenate(
                [prev_ref[:, vcols] if b == 0 else v_ref[before, cols], v_ref[rows, cols]]
                + [glob_ref[g, :, vcols] for g in range(GLOB)],
                axis=0,
            )
            qs = stack_pair(q_ref[rows, cols]) * HEAD_DIM**-0.5
            gs = stack_pair(g_ref[rows, cols])
            scores = dg(qs, kk, NT)
            sig = 0.5 * jnp.tanh(0.5 * scores) + 0.5
            masked = sig * mask
            probs = (scores * masked).astype(BF16)
            slope = masked * (1.0 + scores * (1.0 - sig))
            d_scores = (dg(gs, vv, NT) * slope).astype(BF16)
            dq_ref[rows, cols] = (merge_pair(mm(d_scores, kk)) * HEAD_DIM**-0.5).astype(BF16)
            for grad, at in ((dg(d_scores, qs, TN), cols), (dg(probs, gs, TN), vcols)):
                if b == 0:
                    d_prev_ref[:, at] = grad[:BLK].astype(BF16)
                else:
                    dkv_ref[before, at] += grad[:BLK]
                dkv_ref[rows, at] = grad[BLK : 2 * BLK]
                for g in range(GLOB):
                    piece = grad[(2 + g) * BLK : (3 + g) * BLK]
                    if b == 0:
                        acc_ref[g, :, at] = piece
                    else:
                        acc_ref[g, :, at] += piece
    d_glob_ref[...] = acc_ref[...].astype(BF16)


def call(kernel, outs, in_specs, scratch=(), flops=1 << 30):
    return pl.pallas_call(
        kernel,
        out_shape=[jax.ShapeDtypeStruct(shape, dtype) for shape, dtype in outs],
        in_specs=in_specs,
        out_specs=[VMEM] * len(outs),
        scratch_shapes=list(scratch),
        compiler_params=pltpu.CompilerParams(vmem_limit_bytes=LIMIT),
        cost_estimate=pl.CostEstimate(flops=flops, bytes_accessed=1 << 22, transcendentals=0),
    )


def from_behind(block, axis, distance):
    devices = range(lax.axis_size(axis))
    route = [(i - distance, i) for i in devices if i - distance in devices]
    return lax.ppermute(block, axis, route)


def on_device(
    query, key, value, gate, history, w_out, table, item_owner, item_row, global_blocks, lengths
):
    q, k, v = query[0], key[0], value[0]
    events, width = q.shape
    nbd = events // BLK
    emb = table.shape[1]
    axes = ("seq", "user")
    ndev = lax.axis_size(axes)
    cap = -(-max(2, 15 * events // (2 * ndev)) // 16) * 16
    seq_idx = lax.axis_index("seq")
    length = lax.dynamic_slice_in_dim(lengths, lax.axis_index("user"), 1)[0]
    gids = global_blocks[0]
    base = seq_idx * nbd
    info = jnp.concatenate([jnp.stack([base, length]), gids]).astype(jnp.int32)
    owner_t, row_t = item_owner[0].T, item_row[0].T

    slots, requests = call(
        request_kernel, [((ndev, events), F32), ((ndev, cap), jnp.int32)], [VMEM] * 2
    )(owner_t, row_t)
    asked = lax.all_to_all(requests, axes, split_axis=0, concat_axis=0, tiled=True)

    previous = from_behind(jnp.concatenate([k[events - BLK :], v[events - BLK :]], axis=1), "seq", 1)
    holder, local_block = gids // nbd, gids % nbd
    held = holder == seq_idx
    pieces = jnp.stack(
        [
            jnp.concatenate(
                [lax.dynamic_slice_in_dim(x, local_block[g] * BLK, BLK, 0) for x in (k, v)], axis=1
            )
            for g in range(GLOB)
        ]
    )
    glob = lax.psum(jnp.where(held[:, None, None], pieces, jnp.zeros((), BF16)), "seq")

    asked_t = asked.T
    (found,) = call(gather_kernel, [((ndev, cap, emb), BF16)], [VMEM] * 2)(asked_t, table)
    returned = lax.all_to_all(found, axes, split_axis=0, concat_axis=0, tiled=True)

    (attn,) = call(forward_kernel, [((events, width), F32)], [SMEM] + [VMEM] * 5)(
        info, q, k, v, previous, glob
    )
    d_attn, d_gate, outgoing = call(
        middle_kernel,
        [((events, width), BF16), ((events, width), BF16), ((ndev, cap, emb), BF16)],
        [SMEM] + [VMEM] * 7,
    )(info, attn, gate[0], history[0], w_out, returned, slots, owner_t)
    incoming = lax.all_to_all(outgoing, axes, split_axis=0, concat_axis=0, tiled=True)

    d_q, local, d_prev, d_glob = call(
        backward_kernel,
        [
            ((events, width), BF16),
            ((events, 2 * width), F32),
            ((BLK, 2 * width), BF16),
            ((GLOB, BLK, 2 * width), BF16),
        ],
        [SMEM] + [VMEM] * 6,
        [pltpu.VMEM((GLOB, BLK, 2 * width), F32)],
    )(info, q, k, v, previous, glob, d_attn)
    edge = from_behind(d_prev, "seq", -1).astype(F32)
    glob_total = lax.psum(d_glob, "seq").astype(F32)
    blocks = local.reshape(nbd, BLK, 2 * width).at[nbd - 1].add(edge)
    here = (jnp.arange(nbd)[:, None] == local_block[None, :]) & held[None, :]
    for g in range(GLOB):
        blocks = blocks + jnp.where(here[:, g, None, None], glob_total[g][None], 0.0)
    local = blocks.reshape(events, 2 * width).astype(BF16)

    (table_grad,) = call(scatter_kernel, [(table.shape, F32)], [VMEM] * 3)(
        asked_t, asked.reshape(1, ndev * cap), incoming
    )
    return (d_q[None], local[None, :, :width], local[None, :, width:], d_gate[None], table_grad)


def solution(mesh):
    return jax.shard_map(
        on_device,
        mesh=mesh,
        in_specs=(
            P("user", "seq", None),
            P("user", "seq", None),
            P("user", "seq", None),
            P("user", "seq", None),
            P("user", "seq", None),
            P(),
            P(("seq", "user"), None),
            P("user", "seq", None),
            P("user", "seq", None),
            P("user", None),
            P(),
        ),
        out_specs=(
            P("user", "seq", None),
            P("user", "seq", None),
            P("user", "seq", None),
            P("user", "seq", None),
            P(("seq", "user"), None),
        ),
        check_vma=False,
    )
```

```python
import functools

import jax
import jax.numpy as jnp
from jax import lax
from jax.experimental import pallas as pl
from jax.experimental.pallas import tpu as pltpu
from jax.sharding import PartitionSpec as P

HEADS = 8
HEAD_DIM = 64
BLK = 128
GLOB = 2
PAIR = 2 * HEAD_DIM
HI = 512
F32 = jnp.float32
BF16 = jnp.bfloat16
VMEM = pl.BlockSpec(memory_space=pltpu.VMEM)
SMEM = pl.BlockSpec(memory_space=pltpu.SMEM)
NT = (((1,), (1,)), ((), ()))
TN = (((0,), (0,)), ((), ()))
LIMIT = 50 * 1024 * 1024


def iota(shape, axis):
    return lax.broadcasted_iota(jnp.int32, shape, axis)


def mm(left, right):
    return jnp.dot(left, right, preferred_element_type=F32)


def dg(left, right, dims):
    return lax.dot_general(left, right, dims, preferred_element_type=F32)


def stack_pair(rows):
    lane = iota(rows.shape, 1)
    zero = jnp.zeros_like(rows)
    return jnp.concatenate(
        [jnp.where(lane < HEAD_DIM, rows, zero), jnp.where(lane < HEAD_DIM, zero, rows)], axis=0
    )


def merge_pair(stacked):
    half = stacked.shape[0] // 2
    lane = iota((half, stacked.shape[1]), 1)
    return jnp.where(lane < HEAD_DIM, stacked[:half], stacked[half:])


def sigmoid(x):
    return 0.5 * jnp.tanh(0.5 * x) + 0.5


def visible(block, length, gids):
    query = iota((2 * BLK, BLK), 0) % BLK
    key = iota((2 * BLK, BLK), 1)
    prev = (key + (block - 1) * BLK < length) & (block > 0)
    own = (key <= query) & (key + block * BLK < length)
    globs = [(key + gid * BLK < length) & (gid < block - 1) for gid in gids]
    return jnp.concatenate([m.astype(F32) for m in [prev, own] + globs], axis=1)


def make_requests(owner_ref, row_ref, ndev, cap):
    events = owner_ref.shape[1]
    dev = iota((ndev, events), 0)
    hits = [owner_ref[j : j + 1, :] == dev for j in range(owner_ref.shape[0])]
    named = functools.reduce(jnp.logical_or, hits)
    upper = (iota((events, events), 0) < iota((events, events), 1)).astype(BF16)
    rank = mm(named.astype(BF16), upper)
    high = jnp.zeros((ndev, cap), F32)
    low = jnp.zeros((ndev, cap), F32)
    place = iota((cap, events), 0)
    for j, hit in enumerate(hits):
        slot = jnp.sum(jnp.where(hit, rank, 0.0), axis=0, keepdims=True).astype(jnp.int32)
        chosen = (place == slot).astype(BF16)
        code = row_ref[j : j + 1, :] + 1
        high += dg(jnp.where(hit, (code // 64).astype(F32), 0.0).astype(BF16), chosen, NT)
        low += dg(jnp.where(hit, (code % 64).astype(F32), 0.0).astype(BF16), chosen, NT)
    requests = (high * 64.0 + low).astype(jnp.int32) - 1
    return jnp.where(named, rank, -1.0).astype(jnp.int32), requests


def column(row):
    n = row.shape[1]
    eye = iota((n, n), 0) == iota((n, n), 1)
    return jnp.sum(jnp.where(eye, row.astype(F32), 0.0), axis=1, keepdims=True).astype(jnp.int32)


def kernel(
    nseq, nuser,
    info_ref, q_ref, k_ref, v_ref, gate_ref, hist_ref, w_ref, table_ref, owner_ref, row_ref,
    dq_ref, dk_ref, dv_ref, d_gate_ref, table_grad_ref,
    ask_out, asked, found, returned, outgoing, incoming, slots_ref, score_ref, weights,
    kv, prev, pieces, rs_in, glob, d_kv, d_glob, d_pieces, rs2_in, glob2, d_prev, edge,
    attn_ref, d_attn_ref, normed_ref,
    req_sems, found_sems, out_sems, prev_sems, edge_sems, rs_sems, ag_sems, rs2_sems, ag2_sems,
):
    ndev = nseq * nuser
    events, width = q_ref.shape
    nbd = events // BLK
    cap, emb = found.shape[1:]
    part_rows = GLOB * BLK // nseq
    s, u = lax.axis_index("seq"), lax.axis_index("user")
    me = s * nuser + u
    base = s * nbd
    length = info_ref[0]
    gids = [info_ref[1 + g] for g in range(GLOB)]

    def remote(src, dst, sems, to):
        return pltpu.make_async_remote_copy(
            src_ref=src, dst_ref=dst, send_sem=sems.at[0], recv_sem=sems.at[1],
            device_id=to, device_id_type=pl.DeviceIdType.MESH,
        )

    def device(d):
        return (d // nuser, lax.rem(d, nuser))

    def peer(i):
        return lax.rem(s + i, nseq)

    def every(n, act):
        lax.fori_loop(0, n, lambda i, _: (act(i), 0)[1], 0)

    def bulk(ref, sems):
        return remote(ref, ref, sems, (lax.rem(s + 1, nseq), u))

    barrier = pltpu.get_barrier_semaphore()

    def greet(i):
        pl.semaphore_signal(
            barrier, inc=1, device_id=device(lax.rem(me + i + 1, ndev)),
            device_id_type=pl.DeviceIdType.MESH,
        )

    every(ndev - 1, greet)
    slots, requests = make_requests(owner_ref, row_ref, ndev, cap)
    slots_ref[...] = slots
    for d in range(ndev):
        ask_out[d] = requests[d : d + 1]
    kv[BLK:, :width] = k_ref[...]
    kv[BLK:, width:] = v_ref[...]
    for g in range(GLOB):
        piece = jnp.zeros((BLK, 2 * width), F32)
        for b in range(nbd):
            held = (gids[g] == base + b).astype(F32)
            piece += kv[(b + 1) * BLK : (b + 2) * BLK, :].astype(F32) * held
        pieces[g * BLK : (g + 1) * BLK, :] = piece.astype(BF16)
    pl.semaphore_wait(barrier, ndev - 1)

    def ask(i):
        d = lax.rem(me + i + 1, ndev)
        remote(ask_out.at[d], asked.at[me], req_sems, device(d)).start()

    every(ndev - 1, ask)
    previous = remote(kv.at[pl.ds(events, BLK)], prev, prev_sems, (lax.rem(s + 1, nseq), u))
    pl.when(s < nseq - 1)(previous.start)

    def scatter_piece(src, dst, sems):
        def send(i):
            to = peer(i + 1)
            rows = pl.ds(pl.multiple_of(to * part_rows, part_rows), part_rows)
            remote(src.at[rows], dst.at[s], sems, (to, u)).start()

        every(nseq - 1, send)

    def share_piece(src, landed, sems_in, whole, sems_out):
        bulk(landed.at[pl.ds(0, nseq - 1)], sems_in).wait_recv()
        mine = pl.ds(pl.multiple_of(s * part_rows, part_rows), part_rows)
        landed[s] = src[mine, :]
        total = landed[0].astype(F32)
        for i in range(1, nseq):
            total += landed[i].astype(F32)
        whole[mine, :] = total.astype(BF16)

        def send(i):
            remote(whole.at[mine], whole.at[mine], sems_out, (peer(i + 1), u)).start()

        every(nseq - 1, send)

    scatter_piece(pieces, rs_in, rs_sems)
    asked[me] = ask_out[me]
    bulk(asked.at[pl.ds(0, ndev - 1)], req_sems).wait_recv()

    table_parts = table_ref.shape[0] // HI

    def rows_for(d):
        want = column(asked[d])
        part = want // HI
        chosen = (jnp.broadcast_to(want - part * HI, (cap, HI)) == iota((cap, HI), 1)).astype(BF16)
        part_b = jnp.broadcast_to(part, (cap, emb))
        rows = jnp.zeros((cap, emb), F32)
        for k in range(table_parts):
            rows = jnp.where(part_b == k, mm(chosen, table_ref[k * HI : (k + 1) * HI, :]), rows)
        return rows.astype(BF16)

    def answer(i):
        d = lax.rem(me + i, ndev)
        found[d] = rows_for(d)
        remote(found.at[d], returned.at[me], found_sems, device(d)).start()

    near = ndev // 4

    def far_first(act):
        every(ndev // 2, lambda i: act(i + near))

    def near_last(act):
        every(near, lambda i: act(i + near + ndev // 2))
        every(near - 1, lambda i: act(i + 1))

    far_first(answer)
    share_piece(pieces, rs_in, rs_sems, glob, ag_sems)
    near_last(answer)
    returned[me] = rows_for(me)

    @pl.when(s > 0)
    def _():
        previous.wait_recv()

    @pl.when(s == 0)
    def _():
        prev[...] = jnp.zeros_like(prev)

    kv[:BLK, :] = prev[...]
    bulk(glob.at[pl.ds(0, (nseq - 1) * part_rows)], ag_sems).wait_recv()

    def at(b, count):
        return pl.ds(pl.multiple_of(b * BLK, BLK), count)

    def keys(b, p):
        cols = slice(p * PAIR, (p + 1) * PAIR)
        return jnp.concatenate([kv[at(b, 2 * BLK), cols], glob[:, cols]], axis=0)

    pairs = width // PAIR

    def forward(b):
        mask = visible(base + b, length, gids)
        for p in range(pairs):
            cols = slice(p * PAIR, (p + 1) * PAIR)
            qs = stack_pair(q_ref[at(b, BLK), cols]) * HEAD_DIM**-0.5
            scores = dg(qs, keys(b, p), NT)
            probs = (scores * sigmoid(scores) * mask).astype(BF16)
            attn_ref[at(b, BLK), cols] = merge_pair(mm(probs, keys(b, pairs + p)))

    every(nbd, forward)

    attn = attn_ref[...]
    centered = attn - jnp.mean(attn, axis=1, keepdims=True)
    inv = lax.rsqrt(jnp.mean(centered * centered, axis=1, keepdims=True) + 1e-05)
    normed = centered * inv
    normed_ref[...] = normed
    gate = gate_ref[...].astype(F32)
    user = mm((normed * gate).astype(BF16), w_ref[...]) + hist_ref[...].astype(F32)
    user_hi = user.astype(BF16)
    user_lo = (user - user_hi.astype(F32)).astype(BF16)
    user_both = jnp.concatenate([user_hi, user_lo], axis=1)
    place = iota((cap, events), 0)

    bulk(returned.at[pl.ds(0, ndev - 1)], found_sems).wait_recv()

    def score_of(i):
        for k in range(4):
            d = i * 4 + k
            rows = returned[d]
            full = dg(jnp.concatenate([rows, rows], axis=1), user_both, NT)
            here = place == slots_ref[pl.ds(d, 1), :]
            score_ref[pl.ds(d, 1), :] = jnp.sum(jnp.where(here, full, 0.0), axis=0, keepdims=True)

    every(ndev // 4, score_of)
    score = score_ref[...]
    positive = owner_ref[0:1, :] == iota((ndev, events), 0)
    first = jnp.sum(jnp.where(positive, score, 0.0), axis=0, keepdims=True)
    valid = base * BLK + iota((ndev, events), 1) < length
    side = jnp.where(
        (slots_ref[...] >= 0) & valid & ~positive, sigmoid(score - first), 0.0
    )
    score_ref[...] = jnp.where(positive, -jnp.sum(side, axis=0, keepdims=True), side)

    def weigh(d):
        here = place == slots_ref[pl.ds(d, 1), :]
        part = jnp.where(here, score_ref[pl.ds(d, 1), :], 0.0).astype(BF16)
        weights[pl.ds(pl.multiple_of(d * cap, cap), cap), :] = part
        return mm(part, user_hi).astype(BF16)

    def give(i):
        d = lax.rem(me + i, ndev)
        outgoing[d] = weigh(d)
        remote(outgoing.at[d], incoming.at[me], out_sems, device(d)).start()

    far_first(give)
    near_last(give)
    incoming[me] = weigh(me)
    d_user = dg(returned[...].reshape(ndev * cap, emb), weights[...], TN)
    d_gated = dg(d_user.T.astype(BF16), w_ref[...], NT)
    normed = normed_ref[...]
    d_gate_ref[...] = (d_gated * normed).astype(BF16)
    dn = d_gated * gate_ref[...].astype(F32)
    shift = jnp.mean(dn, axis=1, keepdims=True)
    d_attn_ref[...] = (
        (dn - shift - normed * jnp.mean(dn * normed, axis=1, keepdims=True)) * inv
    ).astype(BF16)

    d_kv[...] = jnp.zeros_like(d_kv)
    d_glob[...] = jnp.zeros_like(d_glob)

    def backward(b):
        mask = visible(base + b, length, gids)
        for p in range(pairs):
            cols = slice(p * PAIR, (p + 1) * PAIR)
            vcols = slice(width + p * PAIR, width + (p + 1) * PAIR)
            kk = keys(b, p)
            qs = stack_pair(q_ref[at(b, BLK), cols]) * HEAD_DIM**-0.5
            gs = stack_pair(d_attn_ref[at(b, BLK), cols])
            scores = dg(qs, kk, NT)
            sig = sigmoid(scores)
            masked = sig * mask
            probs = (scores * masked).astype(BF16)
            slope = masked * (1.0 + scores * (1.0 - sig))
            d_scores = (dg(gs, keys(b, pairs + p), NT) * slope).astype(BF16)
            dq_ref[at(b, BLK), cols] = (merge_pair(mm(d_scores, kk)) * HEAD_DIM**-0.5).astype(BF16)
            for grad, to in ((dg(d_scores, qs, TN), cols), (dg(probs, gs, TN), vcols)):
                d_kv[at(b, 2 * BLK), to] += grad[: 2 * BLK]
                d_glob[:, to] += grad[2 * BLK :]

    every(nbd, backward)
    d_pieces[...] = d_glob[...].astype(BF16)
    scatter_piece(d_pieces, rs2_in, rs2_sems)
    d_prev[...] = d_kv[:BLK, :].astype(BF16)
    back = remote(d_prev, edge, edge_sems, (lax.rem(s + nseq - 1, nseq), u))
    pl.when(s > 0)(back.start)

    group = 512 // cap
    bulk(incoming.at[pl.ds(0, ndev - 1)], out_sems).wait_recv()
    table_grad_ref[...] = jnp.zeros_like(table_grad_ref)

    def add_rows(i):
        wanted, wide = [], []
        for j in range(group):
            d = i * group + j
            wanted.append(asked[d])
            part_b = jnp.broadcast_to(column(asked[d]), (cap, emb)) // HI
            inc = incoming[d].astype(F32)
            kept = [jnp.where(part_b == k, inc, 0.0).astype(BF16) for k in range(table_parts)]
            wide.append(jnp.concatenate(kept, axis=1))
        row = jnp.concatenate(wanted, axis=1)
        chosen = (row % HI == iota((HI, group * cap), 0)).astype(BF16)
        total = mm(chosen, jnp.concatenate(wide, axis=0))
        for k in range(table_parts):
            table_grad_ref[k * HI : (k + 1) * HI, :] += total[:, k * emb : (k + 1) * emb]

    steps = ndev // group
    every(steps // 2, add_rows)
    share_piece(d_pieces, rs2_in, rs2_sems, glob2, ag2_sems)
    every(steps - steps // 2, lambda i: add_rows(i + steps // 2))

    @pl.when(s < nseq - 1)
    def _():
        back.wait_recv()

    @pl.when(s == nseq - 1)
    def _():
        edge[...] = jnp.zeros_like(edge)

    d_kv[events:, :] += edge[...].astype(F32)
    bulk(glob2.at[pl.ds(0, (nseq - 1) * part_rows)], ag2_sems).wait_recv()
    for b in range(nbd):
        total = d_kv[(b + 1) * BLK : (b + 2) * BLK, :]
        for g in range(GLOB):
            held = (gids[g] == base + b).astype(F32)
            total += glob2[g * BLK : (g + 1) * BLK, :].astype(F32) * held
        dk_ref[b * BLK : (b + 1) * BLK, :] = total[:, :width].astype(BF16)
        dv_ref[b * BLK : (b + 1) * BLK, :] = total[:, width:].astype(BF16)

    pl.when(s < nseq - 1)(previous.wait_send)
    pl.when(s > 0)(back.wait_send)
    for ref, sems, count in (
        (ask_out, req_sems, ndev - 1),
        (found, found_sems, ndev - 1),
        (outgoing, out_sems, ndev - 1),
        (rs_in, rs_sems, nseq - 1),
        (rs2_in, rs2_sems, nseq - 1),
        (glob, ag_sems, (nseq - 1) * part_rows),
        (glob2, ag2_sems, (nseq - 1) * part_rows),
    ):
        bulk(ref.at[pl.ds(0, count)], sems).wait_send()


def on_device(
    query, key, value, gate, history, w_out, table, item_owner, item_row, global_blocks, lengths
):
    events, width = query.shape[1:]
    emb = table.shape[1]
    nseq, nuser = lax.axis_size("seq"), lax.axis_size("user")
    ndev = nseq * nuser
    cap = -(-max(2, 15 * events // (2 * ndev)) // 16) * 16
    length = lax.dynamic_slice_in_dim(lengths, lax.axis_index("user"), 1)
    info = jnp.concatenate([length, global_blocks[0]]).astype(jnp.int32)
    rows = events + BLK
    part_rows = GLOB * BLK // nseq
    outs = [((events, width), BF16)] * 4 + [(table.shape, F32)]
    scratch = [
        ((ndev, 1, cap), jnp.int32), ((ndev, 1, cap), jnp.int32),
        ((ndev, cap, emb), BF16), ((ndev, cap, emb), BF16),
        ((ndev, cap, emb), BF16), ((ndev, cap, emb), BF16),
        ((ndev, events), jnp.int32), ((ndev, events), F32), ((ndev * cap, events), BF16),
        ((rows, 2 * width), BF16), ((BLK, 2 * width), BF16),
        ((GLOB * BLK, 2 * width), BF16), ((nseq, part_rows, 2 * width), BF16),
        ((GLOB * BLK, 2 * width), BF16),
        ((rows, 2 * width), F32), ((GLOB * BLK, 2 * width), F32),
        ((GLOB * BLK, 2 * width), BF16), ((nseq, part_rows, 2 * width), BF16),
        ((GLOB * BLK, 2 * width), BF16),
        ((BLK, 2 * width), BF16), ((BLK, 2 * width), BF16),
        ((events, width), F32), ((events, width), BF16), ((events, width), F32),
    ]
    d_q, d_k, d_v, d_gate, table_grad = pl.pallas_call(
        functools.partial(kernel, nseq, nuser),
        out_shape=[jax.ShapeDtypeStruct(shape, dtype) for shape, dtype in outs],
        in_specs=[SMEM] + [VMEM] * 9,
        out_specs=[VMEM] * len(outs),
        scratch_shapes=[pltpu.VMEM(shape, dtype) for shape, dtype in scratch]
        + [pltpu.SemaphoreType.DMA((2,))] * 9,
        compiler_params=pltpu.CompilerParams(
            vmem_limit_bytes=LIMIT, collective_id=0, has_side_effects=True
        ),
        cost_estimate=pl.CostEstimate(flops=1 << 33, bytes_accessed=1 << 23, transcendentals=0),
    )(
        info, query[0], key[0], value[0], gate[0], history[0], w_out, table,
        item_owner[0].T, item_row[0].T,
    )
    return (d_q[None], d_k[None], d_v[None], d_gate[None], table_grad)


def solution(mesh):
    return jax.shard_map(
        on_device,
        mesh=mesh,
        in_specs=(
            P("user", "seq", None),
            P("user", "seq", None),
            P("user", "seq", None),
            P("user", "seq", None),
            P("user", "seq", None),
            P(),
            P(("seq", "user"), None),
            P("user", "seq", None),
            P("user", "seq", None),
            P("user", None),
            P(),
        ),
        out_specs=(
            P("user", "seq", None),
            P("user", "seq", None),
            P("user", "seq", None),
            P("user", "seq", None),
            P(("seq", "user"), None),
        ),
        check_vma=False,
    )
```

```python
import functools

import jax
import jax.numpy as jnp
from jax import lax
from jax.experimental import pallas as pl
from jax.experimental.pallas import tpu as pltpu
from jax.sharding import PartitionSpec as P

HEADS = 8
HEAD_DIM = 64
BLK = 128
GLOB = 2
PAIR = 2 * HEAD_DIM
HI = 512
F32 = jnp.float32
BF16 = jnp.bfloat16
VMEM = pl.BlockSpec(memory_space=pltpu.VMEM)
SMEM = pl.BlockSpec(memory_space=pltpu.SMEM)
NT = (((1,), (1,)), ((), ()))
TN = (((0,), (0,)), ((), ()))
LIMIT = 60 * 1024 * 1024


def iota(shape, axis):
    return lax.broadcasted_iota(jnp.int32, shape, axis)


def mm(left, right):
    return jnp.dot(left, right, preferred_element_type=F32)


def dg(left, right, dims):
    return lax.dot_general(left, right, dims, preferred_element_type=F32)


def stack_pair(rows):
    lane = iota(rows.shape, 1)
    zero = jnp.zeros_like(rows)
    return jnp.concatenate(
        [jnp.where(lane < HEAD_DIM, rows, zero), jnp.where(lane < HEAD_DIM, zero, rows)], axis=0
    )


def merge_pair(stacked):
    half = stacked.shape[0] // 2
    lane = iota((half, stacked.shape[1]), 1)
    return jnp.where(lane < HEAD_DIM, stacked[:half], stacked[half:])


def sigmoid(x):
    return 0.5 * jnp.tanh(0.5 * x) + 0.5


def visible(block, length, gids):
    query = iota((2 * BLK, BLK), 0) % BLK
    key = iota((2 * BLK, BLK), 1)
    prev = (key + (block - 1) * BLK < length) & (block > 0)
    own = (key <= query) & (key + block * BLK < length)
    globs = [(key + gid * BLK < length) & (gid < block - 1) for gid in gids]
    return jnp.concatenate([m.astype(F32) for m in [prev, own] + globs], axis=1)


def make_requests(owner_ref, row_ref, ndev, cap):
    events = owner_ref.shape[1]
    dev = iota((ndev, events), 0)
    hits = [owner_ref[j : j + 1, :] == dev for j in range(owner_ref.shape[0])]
    named = functools.reduce(jnp.logical_or, hits)
    upper = (iota((events, events), 0) < iota((events, events), 1)).astype(BF16)
    rank = mm(named.astype(BF16), upper)
    high = jnp.zeros((ndev, cap), F32)
    low = jnp.zeros((ndev, cap), F32)
    place = iota((cap, events), 0)
    for j, hit in enumerate(hits):
        slot = jnp.sum(jnp.where(hit, rank, 0.0), axis=0, keepdims=True).astype(jnp.int32)
        chosen = (place == slot).astype(BF16)
        code = row_ref[j : j + 1, :] + 1
        high += dg(jnp.where(hit, (code // 64).astype(F32), 0.0).astype(BF16), chosen, NT)
        low += dg(jnp.where(hit, (code % 64).astype(F32), 0.0).astype(BF16), chosen, NT)
    requests = (high * 64.0 + low).astype(jnp.int32) - 1
    return jnp.where(named, rank, -1.0).astype(jnp.int32), requests


def column(row):
    n = row.shape[1]
    eye = iota((n, n), 0) == iota((n, n), 1)
    return jnp.sum(jnp.where(eye, row.astype(F32), 0.0), axis=1, keepdims=True).astype(jnp.int32)


def kernel(
    nseq, nuser,
    lengths_ref, gids_ref, q_hbm, k_hbm, v_hbm, gate_hbm, hist_hbm, w_hbm, table_hbm,
    owner_ref, row_ref,
    dq_ref, dk_ref, dv_ref, d_gate_ref, table_grad_ref,
    ask_out, asked, found, returned, outgoing, incoming, slots_ref, score_ref, weights,
    kv, prev, pieces, rs_in, glob, d_kv, d_glob, d_pieces, rs2_in, glob2, d_prev, edge,
    attn_ref, d_attn_ref, normed_ref, q_ref, gate_ref, hist_ref, w_ref, table_ref,
    req_sems, found_sems, out_sems, prev_sems, edge_sems, rs_sems, ag_sems, rs2_sems, ag2_sems,
    found_recv, out_recv, load_sems,
):
    ndev = nseq * nuser
    events, width = q_ref.shape
    nbd = events // BLK
    cap, emb = found.shape[1:]
    part_rows = GLOB * BLK // nseq
    s, u = lax.axis_index("seq"), lax.axis_index("user")
    me = s * nuser + u
    base = s * nbd
    length = lengths_ref[u]
    gids = [gids_ref[0, g] for g in range(GLOB)]

    def remote(src, dst, sems, to, landed=None):
        return pltpu.make_async_remote_copy(
            src_ref=src, dst_ref=dst, send_sem=sems.at[0],
            recv_sem=sems.at[1] if landed is None else landed,
            device_id=to, device_id_type=pl.DeviceIdType.MESH,
        )

    def load(index, src, dst):
        copy = pltpu.make_async_copy(src, dst, load_sems.at[index])
        copy.start()
        return copy

    own = pl.ds(BLK, events)
    load_k = load(0, k_hbm, kv.at[own, pl.ds(0, width)])
    load_v = load(1, v_hbm, kv.at[own, pl.ds(width, width)])
    load_table = load(2, table_hbm, table_ref)
    load_q = load(3, q_hbm, q_ref)
    loads = [
        load(4 + n, src, dst)
        for n, (src, dst) in enumerate(
            [(gate_hbm, gate_ref), (hist_hbm, hist_ref), (w_hbm, w_ref)]
        )
    ]

    def device(d):
        return (d // nuser, lax.rem(d, nuser))

    def peer(i):
        return lax.rem(s + i, nseq)

    def every(n, act):
        lax.fori_loop(0, n, lambda i, _: (act(i), 0)[1], 0)

    def bulk(ref, sems):
        return remote(ref, ref, sems, (lax.rem(s + 1, nseq), u))

    barrier = pltpu.get_barrier_semaphore()

    def greet(i):
        pl.semaphore_signal(
            barrier, inc=1, device_id=device(lax.rem(me + i + 1, ndev)),
            device_id_type=pl.DeviceIdType.MESH,
        )

    every(ndev - 1, greet)
    slots, requests = make_requests(owner_ref, row_ref, ndev, cap)
    slots_ref[...] = slots
    for d in range(ndev):
        ask_out[d] = requests[d : d + 1]
    load_k.wait()
    load_v.wait()
    for g in range(GLOB):
        piece = jnp.zeros((BLK, 2 * width), F32)
        for b in range(nbd):
            held = (gids[g] == base + b).astype(F32)
            piece += kv[(b + 1) * BLK : (b + 2) * BLK, :].astype(F32) * held
        pieces[g * BLK : (g + 1) * BLK, :] = piece.astype(BF16)
    pl.semaphore_wait(barrier, ndev - 1)

    def ask(i):
        d = lax.rem(me + i + 1, ndev)
        remote(ask_out.at[d], asked.at[me], req_sems, device(d)).start()

    every(ndev - 1, ask)
    previous = remote(kv.at[pl.ds(events, BLK)], prev, prev_sems, (lax.rem(s + 1, nseq), u))
    pl.when(s < nseq - 1)(previous.start)

    half = nseq // 2
    mine = pl.ds(pl.multiple_of(s * part_rows, part_rows), part_rows)

    def scatter_piece(src, dst, sems, wanted):
        def send(i):
            to = peer(i + 1)
            rows = pl.ds(pl.multiple_of(to * part_rows, part_rows), part_rows)
            pl.when(wanted(to))(remote(src.at[rows], dst.at[s], sems, (to, u)).start)

        every(nseq - 1, send)

    def add_pieces(src, landed, sems, whole):
        bulk(landed.at[pl.ds(0, nseq - 1)], sems).wait_recv()
        landed[s] = src[mine, :]
        total = landed[0].astype(F32)
        for i in range(1, nseq):
            total += landed[i].astype(F32)
        whole[mine, :] = total.astype(BF16)

    def share_piece(whole, sems, wanted):
        def send(i):
            to = peer(i + 1)
            pl.when(wanted(to))(remote(whole.at[mine], whole.at[mine], sems, (to, u)).start)

        every(nseq - 1, send)

    scatter_piece(pieces, rs_in, rs_sems, lambda to: (to >= half) | (s == 0))
    asked[me] = ask_out[me]
    bulk(asked.at[pl.ds(0, ndev - 1)], req_sems).wait_recv()
    load_table.wait()

    table_parts = table_ref.shape[0] // HI

    def rows_for(d):
        want = column(asked[d])
        part = want // HI
        chosen = (jnp.broadcast_to(want - part * HI, (cap, HI)) == iota((cap, HI), 1)).astype(BF16)
        part_b = jnp.broadcast_to(part, (cap, emb))
        rows = jnp.zeros((cap, emb), F32)
        for k in range(table_parts):
            rows = jnp.where(part_b == k, mm(chosen, table_ref[k * HI : (k + 1) * HI, :]), rows)
        return rows.astype(BF16)

    def answer(i):
        d = lax.rem(me + i, ndev)
        found[d] = rows_for(d)
        remote(found.at[d], returned.at[me], found_sems, device(d), found_recv.at[i]).start()

    near = ndev // 4

    def far_first(act):
        every(ndev // 2, lambda i: act(i + near))

    def near_last(act):
        every(near, lambda i: act(i + near + ndev // 2))
        every(near - 1, lambda i: act(i + 1))

    far_first(answer)

    @pl.when(s >= half)
    def _():
        add_pieces(pieces, rs_in, rs_sems, glob)

    @pl.when((s > 0) & (s < half))
    def _():
        bulk(rs_in.at[pl.ds(0, 1)], rs_sems).wait_recv()
        glob[mine, :] = rs_in[0]

    @pl.when(s == 0)
    def _():
        glob[mine, :] = pieces[mine, :]

    share_piece(glob, ag_sems, lambda to: to >= 0)
    near_last(answer)
    returned[me] = rows_for(me)

    @pl.when(s > 0)
    def _():
        previous.wait_recv()

    @pl.when(s == 0)
    def _():
        prev[...] = jnp.zeros_like(prev)

    kv[:BLK, :] = prev[...]
    bulk(glob.at[pl.ds(0, (nseq - 1) * part_rows)], ag_sems).wait_recv()

    def at(b, count):
        return pl.ds(pl.multiple_of(b * BLK, BLK), count)

    def keys(b, p):
        cols = slice(p * PAIR, (p + 1) * PAIR)
        return jnp.concatenate([kv[at(b, 2 * BLK), cols], glob[:, cols]], axis=0)

    pairs = width // PAIR
    load_q.wait()

    def forward(b):
        mask = visible(base + b, length, gids)
        for p in range(pairs):
            cols = slice(p * PAIR, (p + 1) * PAIR)
            qs = stack_pair(q_ref[at(b, BLK), cols]) * HEAD_DIM**-0.5
            scores = dg(qs, keys(b, p), NT)
            probs = (scores * sigmoid(scores) * mask).astype(BF16)
            attn_ref[at(b, BLK), cols] = merge_pair(mm(probs, keys(b, pairs + p)))

    every(nbd, forward)

    for copy in loads:
        copy.wait()

    attn = attn_ref[...]
    centered = attn - jnp.mean(attn, axis=1, keepdims=True)
    inv = lax.rsqrt(jnp.mean(centered * centered, axis=1, keepdims=True) + 1e-05)
    normed = centered * inv
    normed_ref[...] = normed
    gate = gate_ref[...].astype(F32)
    user = mm((normed * gate).astype(BF16), w_ref[...]) + hist_ref[...].astype(F32)
    user_hi = user.astype(BF16)
    user_lo = (user - user_hi.astype(F32)).astype(BF16)
    user_both = jnp.concatenate([user_hi, user_lo], axis=1)
    place = iota((cap, events), 0)

    def arrivals(step, count, into, sems, landed):
        sources = []
        for k in range(count):
            i = lax.rem(step * count + k + near, ndev)
            d = lax.rem(me - i + ndev, ndev)
            copy = remote(into.at[d], into.at[d], sems, device(d), landed.at[i])
            pl.when(i != 0)(copy.wait_recv)
            sources.append(d)
        return sources

    def score_of(step):
        for d in arrivals(step, 4, returned, found_sems, found_recv):
            rows = returned[d]
            full = dg(jnp.concatenate([rows, rows], axis=1), user_both, NT)
            here = place == slots_ref[pl.ds(d, 1), :]
            score_ref[pl.ds(d, 1), :] = jnp.sum(jnp.where(here, full, 0.0), axis=0, keepdims=True)

    every(ndev // 4, score_of)
    score = score_ref[...]
    positive = owner_ref[0:1, :] == iota((ndev, events), 0)
    first = jnp.sum(jnp.where(positive, score, 0.0), axis=0, keepdims=True)
    valid = base * BLK + iota((ndev, events), 1) < length
    side = jnp.where(
        (slots_ref[...] >= 0) & valid & ~positive, sigmoid(score - first), 0.0
    )
    score_ref[...] = jnp.where(positive, -jnp.sum(side, axis=0, keepdims=True), side)

    def weigh(d):
        here = place == slots_ref[pl.ds(d, 1), :]
        part = jnp.where(here, score_ref[pl.ds(d, 1), :], 0.0).astype(BF16)
        weights[pl.ds(pl.multiple_of(d * cap, cap), cap), :] = part
        return mm(part, user_hi).astype(BF16)

    def give(i):
        d = lax.rem(me + i, ndev)
        outgoing[d] = weigh(d)
        remote(outgoing.at[d], incoming.at[me], out_sems, device(d), out_recv.at[i]).start()

    far_first(give)
    near_last(give)
    incoming[me] = weigh(me)
    d_user = dg(returned[...].reshape(ndev * cap, emb), weights[...], TN)
    d_gated = dg(d_user.T.astype(BF16), w_ref[...], NT)
    normed = normed_ref[...]
    d_gate_ref[...] = (d_gated * normed).astype(BF16)
    dn = d_gated * gate_ref[...].astype(F32)
    shift = jnp.mean(dn, axis=1, keepdims=True)
    d_attn_ref[...] = (
        (dn - shift - normed * jnp.mean(dn * normed, axis=1, keepdims=True)) * inv
    ).astype(BF16)

    d_kv[...] = jnp.zeros_like(d_kv)
    d_glob[...] = jnp.zeros_like(d_glob)

    def backward(b):
        mask = visible(base + b, length, gids)
        for p in range(pairs):
            cols = slice(p * PAIR, (p + 1) * PAIR)
            vcols = slice(width + p * PAIR, width + (p + 1) * PAIR)
            kk = keys(b, p)
            qs = stack_pair(q_ref[at(b, BLK), cols]) * HEAD_DIM**-0.5
            gs = stack_pair(d_attn_ref[at(b, BLK), cols])
            scores = dg(qs, kk, NT)
            sig = sigmoid(scores)
            masked = sig * mask
            probs = (scores * masked).astype(BF16)
            slope = masked * (1.0 + scores * (1.0 - sig))
            d_scores = (dg(gs, keys(b, pairs + p), NT) * slope).astype(BF16)
            dq_ref[at(b, BLK), cols] = (merge_pair(mm(d_scores, kk)) * HEAD_DIM**-0.5).astype(BF16)
            for grad, to in ((dg(d_scores, qs, TN), cols), (dg(probs, gs, TN), vcols)):
                d_kv[at(b, 2 * BLK), to] += grad[: 2 * BLK]
                d_glob[:, to] += grad[2 * BLK :]

    every(nbd, backward)
    d_pieces[...] = d_glob[...].astype(BF16)
    scatter_piece(d_pieces, rs2_in, rs2_sems, lambda to: to >= 0)
    d_prev[...] = d_kv[:BLK, :].astype(BF16)
    back = remote(d_prev, edge, edge_sems, (lax.rem(s + nseq - 1, nseq), u))
    pl.when(s > 0)(back.start)

    group = 512 // cap
    table_grad_ref[...] = jnp.zeros_like(table_grad_ref)

    def add_rows(i):
        wanted, wide = [], []
        for d in arrivals(i, group, incoming, out_sems, out_recv):
            wanted.append(asked[d])
            part_b = jnp.broadcast_to(column(asked[d]), (cap, emb)) // HI
            inc = incoming[d].astype(F32)
            kept = [jnp.where(part_b == k, inc, 0.0).astype(BF16) for k in range(table_parts)]
            wide.append(jnp.concatenate(kept, axis=1))
        row = jnp.concatenate(wanted, axis=1)
        chosen = (row % HI == iota((HI, group * cap), 0)).astype(BF16)
        total = mm(chosen, jnp.concatenate(wide, axis=0))
        for k in range(table_parts):
            table_grad_ref[k * HI : (k + 1) * HI, :] += total[:, k * emb : (k + 1) * emb]

    steps = ndev // group
    early = steps * 3 // 4
    every(early, add_rows)
    add_pieces(d_pieces, rs2_in, rs2_sems, glob2)
    share_piece(glob2, ag2_sems, lambda to: (to == 0) | (s >= half))
    every(steps - early, lambda i: add_rows(i + early))

    @pl.when(s < nseq - 1)
    def _():
        back.wait_recv()

    @pl.when(s == nseq - 1)
    def _():
        edge[...] = jnp.zeros_like(edge)

    d_kv[events:, :] += edge[...].astype(F32)
    upper = nseq - half

    def of_pieces(cond, ref, sems, count, received):
        if count:
            copy = bulk(ref.at[pl.ds(0, count * part_rows)], sems)
            pl.when(cond)(copy.wait_recv if received else copy.wait_send)

    of_pieces(s == 0, glob2, ag2_sems, nseq - 1, True)
    of_pieces((s > 0) & (s < half), glob2, ag2_sems, upper, True)
    of_pieces(s >= half, glob2, ag2_sems, upper - 1, True)

    @pl.when(s == 0)
    def _():
        for b in range(nbd):
            held = (gids[0] == b).astype(F32)
            d_kv[(b + 1) * BLK : (b + 2) * BLK, :] += glob2[:BLK, :].astype(F32) * held

    for b in range(nbd):
        total = d_kv[(b + 1) * BLK : (b + 2) * BLK, :]
        for g in range(1, GLOB):
            held = (gids[g] == base + b).astype(F32)
            total += glob2[g * BLK : (g + 1) * BLK, :].astype(F32) * held
        dk_ref[b * BLK : (b + 1) * BLK, :] = total[:, :width].astype(BF16)
        dv_ref[b * BLK : (b + 1) * BLK, :] = total[:, width:].astype(BF16)

    pl.when(s < nseq - 1)(previous.wait_send)
    pl.when(s > 0)(back.wait_send)
    for ref, sems, count in (
        (ask_out, req_sems, ndev - 1),
        (found, found_sems, ndev - 1),
        (outgoing, out_sems, ndev - 1),
        (rs2_in, rs2_sems, nseq - 1),
        (glob, ag_sems, (nseq - 1) * part_rows),
    ):
        bulk(ref.at[pl.ds(0, count)], sems).wait_send()
    of_pieces(s == 0, pieces, rs_sems, nseq - 1, False)
    of_pieces((s > 0) & (s < half), pieces, rs_sems, upper, False)
    of_pieces(s >= half, pieces, rs_sems, upper - 1, False)
    of_pieces((s > 0) & (s < half), glob2, ag2_sems, 1, False)
    of_pieces(s >= half, glob2, ag2_sems, nseq - 1, False)


def on_device(
    query, key, value, gate, history, w_out, table, item_owner, item_row, global_blocks, lengths
):
    events, width = query.shape[1:]
    emb = table.shape[1]
    nseq, nuser = lax.axis_size("seq"), lax.axis_size("user")
    ndev = nseq * nuser
    cap = -(-max(2, 15 * events // (2 * ndev)) // 16) * 16
    rows = events + BLK
    part_rows = GLOB * BLK // nseq
    outs = [((events, width), BF16)] * 4 + [(table.shape, F32)]
    scratch = [
        ((ndev, 1, cap), jnp.int32), ((ndev, 1, cap), jnp.int32),
        ((ndev, cap, emb), BF16), ((ndev, cap, emb), BF16),
        ((ndev, cap, emb), BF16), ((ndev, cap, emb), BF16),
        ((ndev, events), jnp.int32), ((ndev, events), F32), ((ndev * cap, events), BF16),
        ((rows, 2 * width), BF16), ((BLK, 2 * width), BF16),
        ((GLOB * BLK, 2 * width), BF16), ((nseq, part_rows, 2 * width), BF16),
        ((GLOB * BLK, 2 * width), BF16),
        ((rows, 2 * width), F32), ((GLOB * BLK, 2 * width), F32),
        ((GLOB * BLK, 2 * width), BF16), ((nseq, part_rows, 2 * width), BF16),
        ((GLOB * BLK, 2 * width), BF16),
        ((BLK, 2 * width), BF16), ((BLK, 2 * width), BF16),
        ((events, width), F32), ((events, width), BF16), ((events, width), F32),
        ((events, width), BF16), ((events, width), BF16), ((events, emb), BF16),
        (w_out.shape, BF16), (table.shape, BF16),
    ]
    d_q, d_k, d_v, d_gate, table_grad = pl.pallas_call(
        functools.partial(kernel, nseq, nuser),
        out_shape=[jax.ShapeDtypeStruct(shape, dtype) for shape, dtype in outs],
        in_specs=[SMEM] * 2 + [pl.BlockSpec(memory_space=pl.ANY)] * 7 + [VMEM] * 2,
        out_specs=[VMEM] * len(outs),
        scratch_shapes=[pltpu.VMEM(shape, dtype) for shape, dtype in scratch]
        + [pltpu.SemaphoreType.DMA((2,))] * 9
        + [pltpu.SemaphoreType.DMA((n,)) for n in (ndev, ndev, 7)],
        compiler_params=pltpu.CompilerParams(
            vmem_limit_bytes=LIMIT, collective_id=0, has_side_effects=True
        ),
        cost_estimate=pl.CostEstimate(flops=1 << 33, bytes_accessed=1 << 23, transcendentals=0),
    )(
        lengths, global_blocks, query[0], key[0], value[0], gate[0], history[0], w_out, table,
        item_owner[0].T, item_row[0].T,
    )
    return (d_q[None], d_k[None], d_v[None], d_gate[None], table_grad)


def solution(mesh):
    return jax.shard_map(
        on_device,
        mesh=mesh,
        in_specs=(
            P("user", "seq", None),
            P("user", "seq", None),
            P("user", "seq", None),
            P("user", "seq", None),
            P("user", "seq", None),
            P(),
            P(("seq", "user"), None),
            P("user", "seq", None),
            P("user", "seq", None),
            P("user", None),
            P(),
        ),
        out_specs=(
            P("user", "seq", None),
            P("user", "seq", None),
            P("user", "seq", None),
            P("user", "seq", None),
            P(("seq", "user"), None),
        ),
        check_vma=False,
    )
```
